32 devices in a mesh: row: 4 (over z), col: 8 (over y, x, core).
Axes of the slice: x: 2, y: 2, z: 4, core: 2. Of those that a mesh axis runs over, the one named last changes fastest.
Arguments:
- tokens: bfloat16 [128, 4096], P(('row', 'col')), may hold values from -24 to 24
- counts: int32 [32], P(('row', 'col')), may hold values from 1 to 4, 104 in all
- cotangent: bfloat16 [128, 4096], P(('row', 'col')), may hold values from -6 to 6
- up_weight: bfloat16 [2, 4096, 16384], P(None, 'col', 'row'), may hold values from -0.09375 to 0.09375
- down_weight: bfloat16 [2, 16384, 4096], P(None, 'row', 'col'), may hold values from -0.046875 to 0.046875
- norm_gain: float32 [2, 4096], P(None, 'col'), may hold values from 0.5 to 2
Outputs:
- token_grad: bfloat16 [128, 4096], P(('row', 'col'))
- up_grad: float32 [2, 4096, 16384], P(None, 'col', 'row')
- down_grad: float32 [2, 16384, 4096], P(None, 'row', 'col')
- gain_grad: float32 [2, 4096], P(None, 'col')
The draws below stay inside these ranges and needn't reach their ends.
All inputs are finite; a program needn't handle non-finite values. No bound on the sum of `counts` on one device may be relied on, other than what follows from the above.
Results may differ from the reference program's by a relative error of at most 0.0095.
Values may be sent and summed in bfloat16 or wider, within the bound.
A program may use at most 128 MiB of HBM per device.

```python
import math
import jax
import jax.numpy as jnp
import numpy as np
from jax import lax

D = 4096
FF = 16384
LAYERS = 2
SLOTS = 4
TILES = 32
TOKENS = 128


def draw_tokens(key, part):
    key_noise, key_rows = jax.random.split(key, 2)
    columns = jnp.arange(D, dtype=jnp.float32) / D
    column_scale = jnp.exp(jnp.log(0.4) + jnp.log(10.0) * columns)[None, :]
    noise_part = jnp.clip(jax.random.normal(key_noise, (TOKENS, D), jnp.float32), -6.0, 6.0)
    row_scale = jnp.exp(jax.random.uniform(key_rows, (TOKENS, 1), jnp.float32, jnp.log(0.1), jnp.log(1.0)))
    values = noise_part * row_scale * column_scale
    return values.astype(jnp.bfloat16)


def shard_levels(own_key, extent, cuts, low, top_value):
    def one(axis_at, parts):
        draws = jax.random.uniform(jax.random.fold_in(jax.random.fold_in(own_key, 6), axis_at), (parts,), jnp.float32, low / len(cuts), top_value / len(cuts))
        return jnp.repeat(jnp.exp(draws), extent[axis_at] // parts).reshape((-1,) + (1,) * (len(extent) - axis_at - 1))

    level = one(*cuts[0])
    for cut in cuts[1:]:
        level = level * one(*cut)
    return level


def split_up(number_of, total, reach, slope):
    weights = [(1 << 20) // math.isqrt(grade ** slope) + 1 for grade in range(2, number_of + 1)]
    surplus, holding = total - reach - (number_of - 1), [1] * (number_of - 1)
    while surplus > 0:
        candidates = [i for i in range(number_of - 1) if holding[i] < reach]
        pool, remaining = sum([weights[i] for i in candidates]), surplus
        for i in candidates:
            extra = min(reach - holding[i], max(1, remaining * weights[i] // pool), surplus)
            holding[i] = holding[i] + extra
            surplus = surplus - extra
    return np.array([reach] + holding)


def ragged(stream_key, count, total, limit, lean):
    if count == 2:
        one = jax.random.randint(stream_key, (), max(1, total - limit), min(limit, total - 1) + 1)
        return jnp.stack([one, total - one])
    lengths = jnp.asarray(split_up(count, total, limit, lean), jnp.int32)
    twos = (count - 1) // 2
    giver, sink = lengths[1:1 + 2 * twos:2], lengths[2:2 + 2 * twos:2]
    margin = jnp.minimum(giver - 1, limit - sink)
    passed = jax.random.randint(jax.random.fold_in(stream_key, 1), (twos,), 0, 1 << 20) % (margin + 1)
    lengths = lengths.at[1:1 + 2 * twos:2].set(giver - passed).at[2:2 + 2 * twos:2].set(sink + passed)
    return lengths[jax.random.permutation(jax.random.fold_in(stream_key, 2), count)]


def normal_values(rng, shape, scale, limit, cuts=(), held_as=jnp.bfloat16):
    entries = jax.random.normal(rng, shape, jnp.float32) * scale
    if len(cuts) > 0:
        entries = shard_levels(rng, shape, cuts, -0.22, 0.18) * entries
    return jnp.clip(entries, min=-limit, max=limit).astype(held_as)


def setup_inputs(seed: int = 0) -> dict:
    key_list = jax.random.split(jax.random.key(seed), 7)
    tokens = draw_tokens(jax.random.fold_in(key_list[6], 71), 0)
    counts = ragged(key_list[1], TILES, TILES * SLOTS - (TILES // 4) * (SLOTS - 1), SLOTS, 1).astype(jnp.int32)
    cotangent = normal_values(key_list[2], (TOKENS, D), 1.0, 6.0, ((0, 32),))
    up_weight = normal_values(key_list[3], (LAYERS, D, FF), D ** -0.5, 0.09375, ((1, 8), (2, 4)))
    down_weight = normal_values(key_list[4], (LAYERS, FF, D), FF ** -0.5, 0.046875, ((1, 4), (2, 8)))
    norm_gain = jnp.clip(jnp.exp(math.log(2.0) - 1.3862944 * jax.random.uniform(key_list[5], (LAYERS, D), jnp.float32) ** shard_levels(key_list[5], (LAYERS, D), ((1, 8),), -0.2, 0.2)), 0.5, 2.0)
    return {"tokens": tokens, "counts": counts, "cotangent": cotangent, "up_weight": up_weight, "down_weight": down_weight, "norm_gain": norm_gain}


epsilon_norm = 1e-06
gelu_scale = 0.7978845608028654
cubic_term = 0.044715

def gelu_value(pre_act):
    tangent = jnp.tanh(gelu_scale * (pre_act + cubic_term * pre_act * pre_act * pre_act))
    return 0.5 * pre_act * (1.0 + tangent)

def gelu_slope(pre_act):
    tangent = jnp.tanh(gelu_scale * (pre_act + cubic_term * pre_act * pre_act * pre_act))
    return 0.5 * (1.0 + tangent) + 0.5 * pre_act * (1.0 - tangent * tangent) * gelu_scale * (1.0 + 3.0 * cubic_term * pre_act * pre_act)

def reference(tokens, counts, cotangent, up_weight, down_weight, norm_gain):
    positions = jnp.arange(TOKENS, dtype=jnp.int32)
    live_rows = (positions % SLOTS < counts[positions // SLOTS]).astype(jnp.float32)[:, None]
    stream = tokens.astype(jnp.float32)
    saved = []
    for layer_index in range(LAYERS):
        scale_rows = lax.rsqrt(lax.optimization_barrier(jnp.mean(stream * stream, axis=1, keepdims=True)) + epsilon_norm)
        normed = (stream * scale_rows * norm_gain[layer_index][None, :]).astype(jnp.bfloat16)
        pre_act = jnp.dot(normed, up_weight[layer_index], preferred_element_type=jnp.float32)
        hidden = gelu_value(pre_act).astype(jnp.bfloat16)
        saved.append((stream, scale_rows, normed, hidden, pre_act))
        stream = stream + jnp.dot(hidden, down_weight[layer_index], preferred_element_type=jnp.float32)
    grad_stream = cotangent.astype(jnp.float32) * live_rows
    up_grads = []
    down_grads = []
    gain_grads = []
    for layer_index in reversed(range(LAYERS)):
        stream_in, scale_rows, normed, hidden, pre_act = saved[layer_index]
        grad_bf = grad_stream.astype(jnp.bfloat16)
        down_grads.append(jnp.dot(hidden.T, grad_bf, preferred_element_type=jnp.float32))
        grad_hidden = jnp.dot(grad_bf, down_weight[layer_index].T, preferred_element_type=jnp.float32)
        grad_pre = (grad_hidden * gelu_slope(pre_act)).astype(jnp.bfloat16)
        up_grads.append(jnp.dot(normed.T, grad_pre, preferred_element_type=jnp.float32))
        grad_normed = jnp.dot(grad_pre, up_weight[layer_index].T, preferred_element_type=jnp.float32)
        unit_rows = stream_in * scale_rows
        gain_grads.append(lax.optimization_barrier(jnp.sum(grad_normed * unit_rows, axis=0)))
        weighted = grad_normed * norm_gain[layer_index][None, :]
        inner_mean = lax.optimization_barrier(jnp.mean(weighted * unit_rows, axis=1, keepdims=True))
        grad_stream = grad_stream + scale_rows * (weighted - unit_rows * inner_mean)
    token_grad = grad_stream.astype(jnp.bfloat16)
    return (token_grad, jnp.stack(up_grads[::-1]), jnp.stack(down_grads[::-1]), jnp.stack(gain_grads[::-1]))
```

```python
import functools

import jax
import jax.numpy as jnp
from jax import lax
from jax.experimental import pallas as pl
from jax.experimental.pallas import tpu as pltpu
from jax.sharding import PartitionSpec as P

epsilon_norm = 1e-06
gelu_scale = 0.7978845608028654
cubic_term = 0.044715
BF = jnp.bfloat16
F32 = jnp.float32
MESH = pl.DeviceIdType.MESH


def gelu_parts(v):
    t = jnp.tanh(gelu_scale * (v + cubic_term * v * v * v))
    value = 0.5 * v * (1.0 + t)
    slope = 0.5 * (1.0 + t) + 0.5 * v * (1.0 - t * t) * gelu_scale * (1.0 + 3.0 * cubic_term * v * v)
    return value, slope


def dot_nn(a, b):
    return jnp.dot(a, b, preferred_element_type=F32)


def dot_nt(a, b):
    return lax.dot_general(a, b, (((1,), (1,)), ((), ())), preferred_element_type=F32)


def dot_tn(a, b):
    return lax.dot_general(a, b, (((0,), (0,)), ((), ())), preferred_element_type=F32)


def to_row(column):
    wide = jnp.broadcast_to(column, (column.shape[0], 128))
    return jnp.transpose(wide)[0:8]


def to_column(row):
    return jnp.transpose(jnp.broadcast_to(row[0:1], (128, row.shape[1])))


class Counter:
    def __init__(self):
        self.n = 0

    def take(self, k):
        at = self.n
        self.n += k
        return at


def sem_total(R, C):
    nk = C // 2
    return 4 * 2 * nk + 4 * 2 * nk + 4 * (C - 1) + 2 * R + 3 * R + 2 * R + 3 * R + 64


def layers_kernel(R, C, both, gain, up_h, down_h, normed_o, gradb_o, hid_o, dpre_o, grad_o, gsum_o,
                  up, down, xa, gb, hid, dpre, core_s, core_r, chip_s, chip_r, acc, stats, inner,
                  row_s, row_r, rowx, normed_v, pre_v, slope_v, dh_v, stream_v, wsem, osem, ssem, rsem):
    L, T, Dc = both.shape
    H = up.shape[2]
    Hc = H // C
    Tr = T // R
    D = Dc * C
    nk = C // 2
    r, c = lax.axis_index("row"), lax.axis_index("col")
    k, core = c // 2, c % 2
    sib = k * 2 + (1 - core)
    ids = Counter()
    sends = []

    def chip_peer(m):
        out, b = k, 1
        while b < nk:
            out = out + b * ((m // b) % 2) * (1 - 2 * ((k // b) % 2))
            b *= 2
        return out

    def copy(src, dst, at, **where):
        return pltpu.make_async_remote_copy(src_ref=src, dst_ref=dst, send_sem=ssem.at[at], recv_sem=rsem.at[at],
                                            device_id=where, device_id_type=MESH)

    def send(src, dst, at, **where):
        one = copy(src, dst, at, **where)
        one.start()
        sends.append(one)

    def load(i, src, dst):
        one = pltpu.make_async_copy(src, dst, wsem.at[i])
        one.start()
        return one

    w_up0 = load(0, up_h.at[0], up.at[0])
    w_down1 = load(1, down_h.at[1], down.at[1])
    w_down0 = load(2, down_h.at[0], down.at[0])
    w_up1 = load(3, up_h.at[1], up.at[1])

    barrier = pltpu.get_barrier_semaphore()
    for d in range(1, C):
        pl.semaphore_signal(barrier, inc=1, device_id={"col": (c + d) % C}, device_id_type=MESH)
    for d in range(1, R):
        pl.semaphore_signal(barrier, inc=1, device_id={"row": (r + d) % R}, device_id_type=MESH)
    pl.semaphore_wait(barrier, C - 1 + R - 1)

    outs = []

    def emit(src, dst):
        one = pltpu.make_async_copy(src, dst, osem.at[len(outs)])
        one.start()
        outs.append(one)

    def stat_send(u, value):
        base = ids.take(C)
        stats[u, c] = value
        for d in range(1, C):
            send(stats.at[u, c], stats.at[u, c], base + d, col=(c + d) % C)
        return base

    def stat_sum(u, base):
        for d in range(1, C):
            frm = (c + C - d) % C
            copy(stats.at[u, frm], stats.at[u, frm], base + d, col=frm).wait_recv()
        return jnp.sum(stats[u], axis=0)

    def order():
        return list(range(nk - 1, 0, -1)) + [0]

    def rs_core(u, chunk, m, base):
        core_s[u, m] = chunk(chip_peer(m) * 2 + (1 - core)).astype(BF)
        send(core_s.at[u, m], core_r.at[u, m], base + m, col=sib)

    def rs_own(u, chunk, m, base):
        part = chunk(chip_peer(m) * 2 + core)
        copy(core_s.at[u, m], core_r.at[u, m], base + m, col=sib).wait_recv()
        return part + core_r[u, m].astype(F32)

    def rs_start(u, chunk):
        base = ids.take(2 * nk)
        ms = order()
        rs_core(u, chunk, ms[0], base)
        total = None
        for i, m in enumerate(ms):
            if i + 1 < nk:
                rs_core(u, chunk, ms[i + 1], base)
            total = rs_own(u, chunk, m, base)
            if m:
                chip_s[u, m] = total.astype(BF)
                send(chip_s.at[u, m], chip_r.at[u, m], base + nk + m, col=chip_peer(m) * 2 + core)
        return base, total

    def rs_end(u, base, total):
        for m in order()[:-1]:
            copy(chip_s.at[u, m], chip_r.at[u, m], base + nk + m, col=chip_peer(m) * 2 + core).wait_recv()
            total = total + chip_r[u, m].astype(F32)
        return total

    def ag_start(buf):
        base = ids.take(2 * nk)
        for m in order()[:-1]:
            send(buf.at[c], buf.at[c], base + m, col=chip_peer(m) * 2 + core)
        send(buf.at[c], buf.at[c], base, col=sib)
        return base

    def ag_each(buf, base, use):
        use(c)
        copy(buf.at[sib], buf.at[sib], base, col=sib).wait_recv()
        use(sib)
        for m in range(1, nk):
            peer = chip_peer(m) * 2
            mine, other = peer + core, peer + 1 - core
            copy(buf.at[mine], buf.at[mine], base + m, col=mine).wait_recv()
            send(buf.at[mine], buf.at[mine], base + nk + m, col=sib)
            use(mine)
            copy(buf.at[other], buf.at[other], base + nk + m, col=sib).wait_recv()
            use(other)

    def row_scatter(u, value_ref):
        base = ids.take(R)
        for d in range(1, R):
            peer = (r + d) % R
            row_s[u, d] = value_ref[pl.ds(pl.multiple_of(peer * Tr, Tr), Tr), :].astype(BF)
            send(row_s.at[u, d], row_r.at[u, d], base + d, row=peer)
        return base

    def row_sum(u, base, value_ref):
        total = value_ref[pl.ds(pl.multiple_of(r * Tr, Tr), Tr), :]
        for d in range(1, R):
            copy(row_s.at[u, d], row_r.at[u, d], base + d, row=(r + d) % R).wait_recv()
            total = total + row_r[u, d].astype(F32)
        return total

    def row_gather_start(buf):
        base = ids.take(R)
        for d in range(1, R):
            send(buf.at[r], buf.at[r], base + d, row=(r + d) % R)
        return base

    def row_gather_end(buf, base):
        for d in range(1, R):
            frm = (r + R - d) % R
            copy(buf.at[frm], buf.at[frm], base + d, row=frm).wait_recv()

    def lanes(j):
        return pl.ds(pl.multiple_of(j * Hc, Hc), Hc)

    gain0, gain1 = gain[0:1, :], gain[1:2, :]
    own = pl.ds(pl.multiple_of(r * Tr, Tr), Tr)

    tok = both[0].astype(F32)
    s0 = stat_send(0, to_row(jnp.sum(tok * tok, axis=1, keepdims=True)))
    xa[0] = (tok * gain0).astype(BF)
    w_up0.wait()
    base, total = rs_start(0, lambda j: dot_nn(xa[0], up[0, :, lanes(j)]))
    rstd0 = lax.rsqrt(to_column(stat_sum(0, s0)) / D + epsilon_norm)
    stream_v[0] = rstd0
    normed_v[0] = (both[0].astype(F32) * rstd0[:, 0:1] * gain0).astype(BF)
    emit(normed_v.at[0], normed_o.at[0])
    pre = rs_end(0, base, total) * rstd0[:, 0:1]
    value, slope = gelu_parts(pre)
    hid[0, c] = value.astype(BF)
    a0 = ag_start(hid.at[0])
    pre_v[0] = pre
    slope_v[0] = slope

    w_down1.wait()
    base_d, total_d = rs_start(1, lambda j: dot_nt(both[1], down[1, lanes(j), :]))
    dh_v[...] = total_d

    w_down0.wait()
    acc[...] = jnp.zeros_like(acc)

    def use_hidden(j):
        acc[...] += dot_nn(hid[0, j], down[0, lanes(j), :])

    ag_each(hid.at[0], a0, use_hidden)
    b = row_scatter(0, acc)
    stream1 = both[0, own, :].astype(F32) + row_sum(0, b, acc)
    rowx[0, r] = (stream1 * gain1).astype(BF)
    b = row_gather_start(rowx.at[0])
    emit(hid.at[0], hid_o.at[0])
    dh_v[...] = rs_end(1, base_d, dh_v[...])
    w_up1.wait()
    row_gather_end(rowx.at[0], b)

    xa[1] = rowx[0].reshape(T, Dc)
    raw = xa[1].astype(F32) / gain1
    s1 = stat_send(1, to_row(jnp.sum(raw * raw, axis=1, keepdims=True)))
    base, total = rs_start(2, lambda j: dot_nn(xa[1], up[1, :, lanes(j)]))
    rstd1 = lax.rsqrt(to_column(stat_sum(1, s1)) / D + epsilon_norm)
    stream_v[1] = rstd1
    normed_v[1] = (xa[1].astype(F32) * rstd1[:, 0:1]).astype(BF)
    emit(normed_v.at[1], normed_o.at[1])
    pre = rs_end(2, base, total) * rstd1[:, 0:1]
    value, slope = gelu_parts(pre)
    hid[1, c] = value.astype(BF)

    def backward(l, dhidden, pre, slope, stream_own, grad_above, gain_l, u):
        rounded = (dhidden * slope).astype(BF)
        dpre[l, c] = rounded
        a = ag_start(dpre.at[l])
        s = stat_send(2 + u, to_row(jnp.sum(rounded.astype(F32) * pre, axis=1, keepdims=True)))
        acc[...] = jnp.zeros_like(acc)

        def use(j):
            acc[...] += dot_nt(dpre[l, j], up[l, :, lanes(j)])

        ag_each(dpre.at[l], a, use)
        b = row_scatter(1 + u, acc)
        inner[u, r] = stat_sum(2 + u, s)
        bi = row_gather_start(inner.at[u])
        emit(dpre.at[l], dpre_o.at[l])
        a_late = ag_start(hid.at[1]) if l == 1 else None
        dnormed = row_sum(1 + u, b, acc)
        row_gather_end(inner.at[u], bi)
        stream_v[2 + u] = to_column(jnp.sum(inner[u], axis=0))
        inner_own = stream_v[2 + u, own, :][:, 0:1] / D
        rstd_own = stream_v[l, own, :][:, 0:1]
        unit = stream_own * rstd_own
        gsum_o[l:l + 1, :] = jnp.sum(dnormed * unit, axis=0, keepdims=True)
        return grad_above + rstd_own * (dnormed * gain_l - unit * inner_own), a_late

    top = both[1, own, :].astype(F32)
    grad1, a_late = backward(1, dh_v[...], pre, slope, stream1, top, gain1, 0)
    rowx[1, r] = grad1.astype(BF)
    b = row_gather_start(rowx.at[1])
    ag_each(hid.at[1], a_late, lambda j: None)
    emit(hid.at[1], hid_o.at[1])
    row_gather_end(rowx.at[1], b)
    gb[...] = rowx[1].reshape(T, Dc)
    emit(gb, gradb_o)
    base, total = rs_start(3, lambda j: dot_nt(gb[...], down[0, lanes(j), :]))
    dhidden = rs_end(3, base, total)
    grad0, _ = backward(0, dhidden, pre_v[0], slope_v[0], both[0, own, :].astype(F32), grad1, gain0, 1)
    grad_o[...] = grad0.astype(BF)
    for one in sends:
        one.wait_send()
    for one in outs:
        one.wait()


def run_layers(R, C, both, gain, up, down):
    _, T, Dc = both.shape
    L, _, H = up.shape
    Hc, Tr, nk = H // C, T // R, C // 2
    n = sem_total(R, C)
    any_spec = pl.BlockSpec(memory_space=pl.ANY)
    vm = pl.BlockSpec(memory_space=pltpu.VMEM)
    S = jax.ShapeDtypeStruct
    flops = 2 * T * Dc * H * 7
    return pl.pallas_call(
        functools.partial(layers_kernel, R, C),
        out_shape=(S((L, T, Dc), BF), S((T, Dc), BF), S((L, C, T, Hc), BF), S((L, C, T, Hc), BF),
                   S((Tr, Dc), BF), S((L, Dc), F32)),
        in_specs=[vm, vm, any_spec, any_spec],
        out_specs=(any_spec, any_spec, any_spec, any_spec, vm, vm),
        scratch_shapes=[
            pltpu.VMEM(up.shape, BF), pltpu.VMEM(down.shape, BF),
            pltpu.VMEM((L, T, Dc), BF), pltpu.VMEM((T, Dc), BF),
            pltpu.VMEM((L, C, T, Hc), BF), pltpu.VMEM((L, C, T, Hc), BF),
            pltpu.VMEM((4, nk, T, Hc), BF), pltpu.VMEM((4, nk, T, Hc), BF),
            pltpu.VMEM((4, nk, T, Hc), BF), pltpu.VMEM((4, nk, T, Hc), BF),
            pltpu.VMEM((T, Dc), F32),
            pltpu.VMEM((4, C, 8, T), F32), pltpu.VMEM((2, R, 8, T), F32),
            pltpu.VMEM((3, R, Tr, Dc), BF), pltpu.VMEM((3, R, Tr, Dc), BF),
            pltpu.VMEM((2, R, Tr, Dc), BF),
            pltpu.VMEM((L, T, Dc), BF),
            pltpu.VMEM((1, T, Hc), F32), pltpu.VMEM((1, T, Hc), F32), pltpu.VMEM((T, Hc), F32),
            pltpu.VMEM((4, T, 128), F32),
            pltpu.SemaphoreType.DMA((4,)), pltpu.SemaphoreType.DMA((8,)),
            pltpu.SemaphoreType.DMA((n,)), pltpu.SemaphoreType.DMA((n,)),
        ],
        compiler_params=pltpu.CompilerParams(collective_id=0, has_side_effects=True,
                                             vmem_limit_bytes=56 * 1024 * 1024),
        cost_estimate=pl.CostEstimate(flops=flops, bytes_accessed=2 * up.size * 4, transcendentals=0),
        name="layers",
    )(both, gain, up, down)


def grads_kernel(normed, gradb, hid, dpre, up_g, down_g):
    up_g[0] = dot_tn(normed[0], dpre[0, 0])
    down_g[0] = dot_tn(hid[0, 0], gradb[0])


def run_grads(normed, gradb, hid, dpre):
    L, T, Dc = normed.shape
    _, C, _, Hc = hid.shape
    whole = pl.BlockSpec((1, T, Dc), lambda l, j: (l, 0, 0))
    chunk = pl.BlockSpec((1, 1, T, Hc), lambda l, j: (l, j, 0, 0))
    S = jax.ShapeDtypeStruct
    return pl.pallas_call(
        grads_kernel,
        grid=(L, C),
        out_shape=(S((L, Dc, C * Hc), F32), S((L, C * Hc, Dc), F32)),
        in_specs=[whole, whole, chunk, chunk],
        out_specs=(pl.BlockSpec((1, Dc, Hc), lambda l, j: (l, 0, j)),
                   pl.BlockSpec((1, Hc, Dc), lambda l, j: (l, j, 0))),
        compiler_params=pltpu.CompilerParams(vmem_limit_bytes=32 * 1024 * 1024),
        cost_estimate=pl.CostEstimate(flops=4 * L * T * Dc * C * Hc, bytes_accessed=8 * L * Dc * C * Hc,
                                      transcendentals=0),
        name="grads",
    )(normed, gradb, hid, dpre)


def on_device(R, C, tokens, counts, cotangent, up_weight, down_weight, norm_gain):
    slots = tokens.shape[0]
    live = (jnp.arange(slots, dtype=jnp.int32) < counts[0]).astype(BF)[:, None]
    both = jnp.stack([tokens, cotangent * live])
    both = lax.all_to_all(both, "col", split_axis=2, concat_axis=1, tiled=True)
    both = lax.all_gather(both, "row", axis=1, tiled=True)
    normed, gradb0, hid, dpre, grad0, gsum = run_layers(R, C, both, norm_gain, up_weight, down_weight)
    token_grad = lax.all_to_all(grad0, "col", split_axis=0, concat_axis=1, tiled=True)
    gain_grad = lax.psum(gsum, "row")
    up_g, down_g = run_grads(normed, jnp.stack([gradb0, both[1]]), hid, dpre)
    return token_grad, up_g, down_g, gain_grad


def solution(mesh):
    R, C = mesh.shape["row"], mesh.shape["col"]
    return jax.shard_map(
        functools.partial(on_device, R, C),
        mesh=mesh,
        in_specs=(P(("row", "col"), None), P(("row", "col")), P(("row", "col"), None),
                  P(None, "col", "row"), P(None, "row", "col"), P(None, "col")),
        out_specs=(P(("row", "col"), None), P(None, "col", "row"), P(None, "row", "col"), P(None, "col")),
        check_vma=False,
    )
```

```python
import functools

import jax
import jax.numpy as jnp
from jax import lax
from jax.experimental import pallas as pl
from jax.experimental.pallas import tpu as pltpu
from jax.sharding import PartitionSpec as P

epsilon_norm = 1e-06
gelu_scale = 0.7978845608028654
cubic_term = 0.044715
BF = jnp.bfloat16
F32 = jnp.float32
MESH = pl.DeviceIdType.MESH


def gelu_parts(v):
    t = jnp.tanh(gelu_scale * (v + cubic_term * v * v * v))
    value = 0.5 * v * (1.0 + t)
    slope = 0.5 * (1.0 + t) + 0.5 * v * (1.0 - t * t) * gelu_scale * (1.0 + 3.0 * cubic_term * v * v)
    return value, slope


def dot_nn(a, b):
    return jnp.dot(a, b, preferred_element_type=F32)


def dot_nt(a, b):
    return lax.dot_general(a, b, (((1,), (1,)), ((), ())), preferred_element_type=F32)


def dot_tn(a, b):
    return lax.dot_general(a, b, (((0,), (0,)), ((), ())), preferred_element_type=F32)


def to_row(column):
    wide = jnp.broadcast_to(column, (column.shape[0], 128))
    return jnp.transpose(wide)[0:8]


def to_column(row):
    return jnp.transpose(jnp.broadcast_to(row[0:1], (128, row.shape[1])))


class Counter:
    def __init__(self):
        self.n = 0

    def take(self, k):
        at = self.n
        self.n += k
        return at


def sem_total(R, C):
    nk = C // 2
    return 16 * nk + 6 * C + 12 * R


def layers_kernel(R, C, entry, gain, up_h, down_h, normed_o, gradb_o, hid_o, dpre_o, grad_o, gsum_o,
                  up, down, ent, tokx, topx, fin_s, fin_r, gains, xa, gb, hid, dpre, core_s, core_r, chip_s, chip_r, acc, stats, inner,
                  row_s, row_r, rowx, normed_v, pre_v, slope_v, dh_v, stream_v, wsem, osem, ssem, rsem):
    L, Dc, H = up.shape
    Hc = H // C
    T = xa.shape[1]
    Tr = T // R
    D = Dc * C
    half = entry.shape[0] // 2
    nk = C // 2
    r, c = lax.axis_index("row"), lax.axis_index("col")
    k, core = c // 2, c % 2
    sib = k * 2 + (1 - core)
    ids = Counter()
    sends = []

    def chip_peer(m):
        out, b = k, 1
        while b < nk:
            out = out + b * ((m // b) % 2) * (1 - 2 * ((k // b) % 2))
            b *= 2
        return out

    def copy(src, dst, at, **where):
        return pltpu.make_async_remote_copy(src_ref=src, dst_ref=dst, send_sem=ssem.at[at], recv_sem=rsem.at[at],
                                            device_id=where, device_id_type=MESH)

    def send(src, dst, at, **where):
        one = copy(src, dst, at, **where)
        one.start()
        sends.append(one)

    def load(i, src, dst):
        one = pltpu.make_async_copy(src, dst, wsem.at[i])
        one.start()
        return one

    w_up0 = load(0, up_h.at[0], up.at[0])
    w_down1 = load(1, down_h.at[1], down.at[1])
    w_down0 = load(2, down_h.at[0], down.at[0])
    w_up1 = load(3, up_h.at[1], up.at[1])

    barrier = pltpu.get_barrier_semaphore()
    for d in range(1, C):
        pl.semaphore_signal(barrier, inc=1, device_id={"col": (c + d) % C}, device_id_type=MESH)
    for d in range(1, R):
        pl.semaphore_signal(barrier, inc=1, device_id={"row": (r + d) % R}, device_id_type=MESH)
    pl.semaphore_wait(barrier, C - 1 + R - 1)

    base_e = ids.take(C)

    def features(j):
        return pl.ds(pl.multiple_of(j * Dc, Dc), Dc)

    for d in range(1, C):
        peer = (c + d) % C
        send(entry.at[:, features(peer)], ent.at[c], base_e + d, col=peer)
    ent[c] = entry[:, features(c)]

    outs = []

    def emit(src, dst):
        one = pltpu.make_async_copy(src, dst, osem.at[len(outs)])
        one.start()
        outs.append(one)

    def stat_send(u, value):
        base = ids.take(C)
        stats[u, c] = value
        for d in range(1, C):
            send(stats.at[u, c], stats.at[u, c], base + d, col=(c + d) % C)
        return base

    def stat_sum(u, base):
        for d in range(1, C):
            frm = (c + C - d) % C
            copy(stats.at[u, frm], stats.at[u, frm], base + d, col=frm).wait_recv()
        return jnp.sum(stats[u], axis=0)

    def order():
        return list(range(nk - 1, 0, -1)) + [0]

    def rs_core(u, chunk, m, base):
        core_s[u, m] = chunk(chip_peer(m) * 2 + (1 - core)).astype(BF)
        send(core_s.at[u, m], core_r.at[u, m], base + m, col=sib)

    def rs_own(u, chunk, m, base):
        part = chunk(chip_peer(m) * 2 + core)
        copy(core_s.at[u, m], core_r.at[u, m], base + m, col=sib).wait_recv()
        return part + core_r[u, m].astype(F32)

    def rs_start(u, chunk, later=False):
        base = ids.take(2 * nk)
        ms = order()
        rs_core(u, chunk, ms[0], base)
        total = None
        for i, m in enumerate(ms):
            if i + 1 < nk:
                rs_core(u, chunk, ms[i + 1], base)
            total = rs_own(u, chunk, m, base)
            if m:
                chip_s[u, m] = total.astype(BF)
            if m and not later:
                send(chip_s.at[u, m], chip_r.at[u, m], base + nk + m, col=chip_peer(m) * 2 + core)
        return base, total

    def rs_send(u, base):
        for m in order()[:-1]:
            send(chip_s.at[u, m], chip_r.at[u, m], base + nk + m, col=chip_peer(m) * 2 + core)

    def rs_end(u, base, total):
        for m in order()[:-1]:
            copy(chip_s.at[u, m], chip_r.at[u, m], base + nk + m, col=chip_peer(m) * 2 + core).wait_recv()
            total = total + chip_r[u, m].astype(F32)
        return total

    def ag_start(buf):
        base = ids.take(2 * nk)
        for m in order()[:-1]:
            send(buf.at[c], buf.at[c], base + m, col=chip_peer(m) * 2 + core)
        send(buf.at[c], buf.at[c], base, col=sib)
        return base

    def ag_each(buf, base, use):
        use(c)
        copy(buf.at[sib], buf.at[sib], base, col=sib).wait_recv()
        use(sib)
        for m in range(1, nk):
            peer = chip_peer(m) * 2
            mine, other = peer + core, peer + 1 - core
            copy(buf.at[mine], buf.at[mine], base + m, col=mine).wait_recv()
            send(buf.at[mine], buf.at[mine], base + nk + m, col=sib)
            use(mine)
            copy(buf.at[other], buf.at[other], base + nk + m, col=sib).wait_recv()
            use(other)

    def row_scatter(u, value_ref):
        base = ids.take(R)
        for d in range(1, R):
            peer = (r + d) % R
            row_s[u, d] = value_ref[pl.ds(pl.multiple_of(peer * Tr, Tr), Tr), :].astype(BF)
            send(row_s.at[u, d], row_r.at[u, d], base + d, row=peer)
        return base

    def row_sum(u, base, value_ref):
        total = value_ref[pl.ds(pl.multiple_of(r * Tr, Tr), Tr), :]
        for d in range(1, R):
            copy(row_s.at[u, d], row_r.at[u, d], base + d, row=(r + d) % R).wait_recv()
            total = total + row_r[u, d].astype(F32)
        return total

    def row_gather_start(buf):
        base = ids.take(R)
        for d in range(1, R):
            send(buf.at[r], buf.at[r], base + d, row=(r + d) % R)
        return base

    def row_gather_end(buf, base):
        for d in range(1, R):
            frm = (r + R - d) % R
            copy(buf.at[frm], buf.at[frm], base + d, row=frm).wait_recv()

    def lanes(j):
        return pl.ds(pl.multiple_of(j * Hc, Hc), Hc)

    gain0, gain1 = gain[0:1, :], gain[1:2, :]
    own = pl.ds(pl.multiple_of(r * Tr, Tr), Tr)

    for d in range(1, C):
        frm = (c + C - d) % C
        copy(entry.at[:, features(frm)], ent.at[frm], base_e + d, col=frm).wait_recv()
    first = lax.broadcasted_iota(jnp.int32, (2 * half, Dc), 0) < half
    tok_rows, top_rows = [], []
    for i in range(C // 2):
        low, high = ent[2 * i], ent[2 * i + 1]
        tok_rows.append(jnp.where(first, low, pltpu.roll(high, half, 0)))
        top_rows.append(jnp.where(first, pltpu.roll(low, half, 0), high))
    tok_own = jnp.concatenate(tok_rows, axis=0)
    top = jnp.concatenate(top_rows, axis=0)
    tokx[r] = tok_own.astype(BF)
    b_tok = row_gather_start(tokx)
    topx[r] = top.astype(BF)
    b_top = row_gather_start(topx)
    row_gather_end(tokx, b_tok)

    tok = tokx[...].reshape(T, Dc).astype(F32)
    s0 = stat_send(0, to_row(jnp.sum(tok * tok, axis=1, keepdims=True)))
    xa[0] = (tok * gain0).astype(BF)
    w_up0.wait()
    base, total = rs_start(0, lambda j: dot_nn(xa[0], up[0, :, lanes(j)]))
    row_gather_end(topx, b_top)
    gb[1] = topx[...].reshape(T, Dc)
    emit(gb.at[1], gradb_o.at[1])
    w_down1.wait()
    base_d, total_d = rs_start(1, lambda j: dot_nt(gb[1], down[1, lanes(j), :]), later=True)
    dh_v[...] = total_d
    rstd0 = lax.rsqrt(to_column(stat_sum(0, s0)) / D + epsilon_norm)
    stream_v[0] = rstd0
    normed_v[0] = (tok * rstd0[:, 0:1] * gain0).astype(BF)
    emit(normed_v.at[0], normed_o.at[0])
    pre = rs_end(0, base, total) * rstd0[:, 0:1]
    value, slope = gelu_parts(pre)
    hid[0, c] = value.astype(BF)
    a0 = ag_start(hid.at[0])
    pre_v[0] = pre
    slope_v[0] = slope

    w_down0.wait()
    acc[...] = jnp.zeros_like(acc)

    def use_hidden(j):
        acc[...] += dot_nn(hid[0, j], down[0, lanes(j), :])

    ag_each(hid.at[0], a0, use_hidden)
    b = row_scatter(0, acc)
    rs_send(1, base_d)
    stream1 = tokx[r].astype(F32) + row_sum(0, b, acc)
    rowx[0, r] = (stream1 * gain1).astype(BF)
    b = row_gather_start(rowx.at[0])
    emit(hid.at[0], hid_o.at[0])
    dh_v[...] = rs_end(1, base_d, dh_v[...])
    w_up1.wait()
    row_gather_end(rowx.at[0], b)

    xa[1] = rowx[0].reshape(T, Dc)
    raw = xa[1].astype(F32) / gain1
    s1 = stat_send(1, to_row(jnp.sum(raw * raw, axis=1, keepdims=True)))
    base, total = rs_start(2, lambda j: dot_nn(xa[1], up[1, :, lanes(j)]))
    rstd1 = lax.rsqrt(to_column(stat_sum(1, s1)) / D + epsilon_norm)
    stream_v[1] = rstd1
    normed_v[1] = (xa[1].astype(F32) * rstd1[:, 0:1]).astype(BF)
    emit(normed_v.at[1], normed_o.at[1])
    pre = rs_end(2, base, total) * rstd1[:, 0:1]
    value, slope = gelu_parts(pre)
    hid[1, c] = value.astype(BF)

    def backward(l, dhidden, pre, slope, stream_own, grad_above, gain_l, u):
        rounded = (dhidden * slope).astype(BF)
        dpre[l, c] = rounded
        a = ag_start(dpre.at[l])
        s = stat_send(2 + u, to_row(jnp.sum(rounded.astype(F32) * pre, axis=1, keepdims=True)))
        acc[...] = jnp.zeros_like(acc)

        def use(j):
            acc[...] += dot_nt(dpre[l, j], up[l, :, lanes(j)])

        ag_each(dpre.at[l], a, use)
        b = row_scatter(1 + u, acc)
        inner[u, r] = stat_sum(2 + u, s)
        bi = row_gather_start(inner.at[u])
        emit(dpre.at[l], dpre_o.at[l])
        a_late = ag_start(hid.at[1]) if l == 1 else None
        dnormed = row_sum(1 + u, b, acc)
        row_gather_end(inner.at[u], bi)
        stream_v[2 + u] = to_column(jnp.sum(inner[u], axis=0))
        inner_own = stream_v[2 + u, own, :][:, 0:1] / D
        rstd_own = stream_v[l, own, :][:, 0:1]
        unit = stream_own * rstd_own
        gains[l, r] = jnp.broadcast_to(jnp.sum(dnormed * unit, axis=0, keepdims=True), (8, Dc))
        bg = row_gather_start(gains.at[l])
        return grad_above + rstd_own * (dnormed * gain_l - unit * inner_own), a_late, bg

    grad1, a_late, bg1 = backward(1, dh_v[...], pre, slope, stream1, top, gain1, 0)
    rowx[1, r] = grad1.astype(BF)
    b = row_gather_start(rowx.at[1])
    ag_each(hid.at[1], a_late, lambda j: None)
    emit(hid.at[1], hid_o.at[1])
    row_gather_end(rowx.at[1], b)
    gb[0] = rowx[1].reshape(T, Dc)
    emit(gb.at[0], gradb_o.at[0])
    base, total = rs_start(3, lambda j: dot_nt(gb[0], down[0, lanes(j), :]))
    dhidden = rs_end(3, base, total)
    grad0, _, bg0 = backward(0, dhidden, pre_v[0], slope_v[0], tokx[r].astype(F32), grad1, gain0, 1)

    fin_s[...] = grad0.reshape(C // 2, 2 * half, Dc)
    base_x = ids.take(C)
    for d in range(1, C):
        peer = (c + d) % C
        send(fin_s.at[peer // 2], fin_r.at[c], base_x + d, col=peer)
    fin_r[c] = fin_s[k]
    for l, bg in ((1, bg1), (0, bg0)):
        row_gather_end(gains.at[l], bg)
        gsum_o[l:l + 1, :] = jnp.sum(gains[l], axis=0)[0:1]
    for d in range(1, C):
        frm = (c + C - d) % C
        copy(fin_s.at[k], fin_r.at[frm], base_x + d, col=frm).wait_recv()
    upper = core == 1
    for j in range(C):
        block = fin_r[j]
        block = jnp.where(upper, pltpu.roll(block, half, 0), block)
        grad_o[:, j * Dc:(j + 1) * Dc] = block[0:half].astype(BF)
    for one in sends:
        one.wait_send()
    for one in outs:
        one.wait()


def run_layers(R, C, entry, gain, up, down):
    L, Dc, H = up.shape
    half = entry.shape[0] // 2
    T = half * R * C
    Hc, Tr, nk = H // C, T // R, C // 2
    n = sem_total(R, C)
    any_spec = pl.BlockSpec(memory_space=pl.ANY)
    vm = pl.BlockSpec(memory_space=pltpu.VMEM)
    S = jax.ShapeDtypeStruct
    flops = 2 * T * Dc * H * 7
    return pl.pallas_call(
        functools.partial(layers_kernel, R, C),
        out_shape=(S((L, T, Dc), BF), S((L, T, Dc), BF), S((L, C, T, Hc), BF), S((L, C, T, Hc), BF),
                   S((half, C * Dc), BF), S((L, Dc), F32)),
        in_specs=[vm, vm, any_spec, any_spec],
        out_specs=(any_spec, any_spec, any_spec, any_spec, vm, vm),
        scratch_shapes=[
            pltpu.VMEM(up.shape, BF), pltpu.VMEM(down.shape, BF),
            pltpu.VMEM((C, 2 * half, Dc), F32), pltpu.VMEM((R, Tr, Dc), BF), pltpu.VMEM((R, Tr, Dc), BF),
            pltpu.VMEM((C // 2, 2 * half, Dc), F32), pltpu.VMEM((C, 2 * half, Dc), F32),
            pltpu.VMEM((L, R, 8, Dc), F32),
            pltpu.VMEM((L, T, Dc), BF), pltpu.VMEM((L, T, Dc), BF),
            pltpu.VMEM((L, C, T, Hc), BF), pltpu.VMEM((L, C, T, Hc), BF),
            pltpu.VMEM((4, nk, T, Hc), BF), pltpu.VMEM((4, nk, T, Hc), BF),
            pltpu.VMEM((4, nk, T, Hc), BF), pltpu.VMEM((4, nk, T, Hc), BF),
            pltpu.VMEM((T, Dc), F32),
            pltpu.VMEM((4, C, 8, T), F32), pltpu.VMEM((2, R, 8, T), F32),
            pltpu.VMEM((3, R, Tr, Dc), BF), pltpu.VMEM((3, R, Tr, Dc), BF),
            pltpu.VMEM((2, R, Tr, Dc), BF),
            pltpu.VMEM((L, T, Dc), BF),
            pltpu.VMEM((1, T, Hc), F32), pltpu.VMEM((1, T, Hc), F32), pltpu.VMEM((T, Hc), F32),
            pltpu.VMEM((4, T, 128), F32),
            pltpu.SemaphoreType.DMA((4,)), pltpu.SemaphoreType.DMA((8,)),
            pltpu.SemaphoreType.DMA((n,)), pltpu.SemaphoreType.DMA((n,)),
        ],
        compiler_params=pltpu.CompilerParams(collective_id=0, has_side_effects=True,
                                             vmem_limit_bytes=56 * 1024 * 1024),
        cost_estimate=pl.CostEstimate(flops=flops, bytes_accessed=2 * up.size * 4, transcendentals=0),
        name="layers",
    )(entry, gain, up, down)


def grads_kernel(normed, gradb, hid, dpre, up_g, down_g):
    up_g[0] = dot_tn(normed[0], dpre[0, 0])
    down_g[0] = dot_tn(hid[0, 0], gradb[0])


def run_grads(normed, gradb, hid, dpre):
    L, T, Dc = normed.shape
    _, C, _, Hc = hid.shape
    whole = pl.BlockSpec((1, T, Dc), lambda l, j: (l, 0, 0))
    chunk = pl.BlockSpec((1, 1, T, Hc), lambda l, j: (l, j, 0, 0))
    S = jax.ShapeDtypeStruct
    return pl.pallas_call(
        grads_kernel,
        grid=(L, C),
        out_shape=(S((L, Dc, C * Hc), F32), S((L, C * Hc, Dc), F32)),
        in_specs=[whole, whole, chunk, chunk],
        out_specs=(pl.BlockSpec((1, Dc, Hc), lambda l, j: (l, 0, j)),
                   pl.BlockSpec((1, Hc, Dc), lambda l, j: (l, j, 0))),
        compiler_params=pltpu.CompilerParams(vmem_limit_bytes=60 * 1024 * 1024),
        cost_estimate=pl.CostEstimate(flops=4 * L * T * Dc * C * Hc, bytes_accessed=8 * L * Dc * C * Hc,
                                      transcendentals=0),
        name="grads",
    )(normed, gradb, hid, dpre)


def on_device(R, C, tokens, counts, cotangent, up_weight, down_weight, norm_gain):
    slots = tokens.shape[0]
    live = (jnp.arange(slots, dtype=jnp.int32) < counts[0]).astype(BF)[:, None]
    entry = jnp.concatenate([tokens, cotangent * live]).astype(F32)
    normed, gradb, hid, dpre, token_grad, gain_grad = run_layers(R, C, entry, norm_gain, up_weight, down_weight)
    up_g, down_g = run_grads(normed, gradb, hid, dpre)
    return token_grad, up_g, down_g, gain_grad


def solution(mesh):
    R, C = mesh.shape["row"], mesh.shape["col"]
    return jax.shard_map(
        functools.partial(on_device, R, C),
        mesh=mesh,
        in_specs=(P(("row", "col"), None), P(("row", "col")), P(("row", "col"), None),
                  P(None, "col", "row"), P(None, "row", "col"), P(None, "col")),
        out_specs=(P(("row", "col"), None), P(None, "col", "row"), P(None, "row", "col"), P(None, "col")),
        check_vma=False,
    )
```

```python
import functools

import jax
import jax.numpy as jnp
from jax import lax
from jax.experimental import pallas as pl
from jax.experimental.pallas import tpu as pltpu
from jax.sharding import PartitionSpec as P

epsilon_norm = 1e-06
gelu_scale = 0.7978845608028654
cubic_term = 0.044715
BF = jnp.bfloat16
F32 = jnp.float32
MESH = pl.DeviceIdType.MESH


def gelu_parts(v):
    t = jnp.tanh(gelu_scale * (v + cubic_term * v * v * v))
    value = 0.5 * v * (1.0 + t)
    slope = 0.5 * (1.0 + t) + 0.5 * v * (1.0 - t * t) * gelu_scale * (1.0 + 3.0 * cubic_term * v * v)
    return value, slope


def dot_nn(a, b):
    return jnp.dot(a, b, preferred_element_type=F32)


def dot_nt(a, b):
    return lax.dot_general(a, b, (((1,), (1,)), ((), ())), preferred_element_type=F32)


def dot_tn(a, b):
    return lax.dot_general(a, b, (((0,), (0,)), ((), ())), preferred_element_type=F32)


def to_row(column):
    wide = jnp.broadcast_to(column, (column.shape[0], 128))
    return jnp.transpose(wide)[0:8]


def to_column(row):
    return jnp.transpose(jnp.broadcast_to(row[0:1], (128, row.shape[1])))


class Counter:
    def __init__(self):
        self.n = 0

    def take(self, k):
        at = self.n
        self.n += k
        return at


def sem_total(R, C):
    nk = C // 2
    return 16 * nk + 6 * C + 12 * R


def layers_kernel(R, C, tokens, cotangent, counts, gain, up_h, down_h, normed_o, gradb_o, hid_o, dpre_o, grad_o, gsum_o,
                  up, down, normed_t, hid_t, entry, ent, tokx, topx, fin_s, fin_r, gains, xa, gb, hid, dpre, core_s, core_r, chip_s, chip_r, acc, stats, inner,
                  row_s, row_r, rowx, normed_v, pre_v, slope_v, dh_v, stream_v, wsem, osem, ssem, rsem):
    L, Dc, H = up.shape
    Hc = H // C
    T = xa.shape[1]
    Tr = T // R
    D = Dc * C
    half = tokens.shape[0]
    nk = C // 2
    r, c = lax.axis_index("row"), lax.axis_index("col")
    k, core = c // 2, c % 2
    sib = k * 2 + (1 - core)
    ids = Counter()
    sends = []

    def chip_peer(m):
        out, b = k, 1
        while b < nk:
            out = out + b * ((m // b) % 2) * (1 - 2 * ((k // b) % 2))
            b *= 2
        return out

    def copy(src, dst, at, **where):
        return pltpu.make_async_remote_copy(src_ref=src, dst_ref=dst, send_sem=ssem.at[at], recv_sem=rsem.at[at],
                                            device_id=where, device_id_type=MESH)

    def send(src, dst, at, **where):
        one = copy(src, dst, at, **where)
        one.start()
        sends.append(one)

    def load(i, src, dst):
        one = pltpu.make_async_copy(src, dst, wsem.at[i])
        one.start()
        return one

    w_up0 = load(0, up_h.at[0], up.at[0])
    w_down1 = load(1, down_h.at[1], down.at[1])
    w_down0 = load(2, down_h.at[0], down.at[0])
    w_up1 = load(3, up_h.at[1], up.at[1])

    slot = lax.broadcasted_iota(jnp.int32, cotangent.shape, 0)
    live = jnp.where(slot < counts[0], 1.0, 0.0)
    entry[0:half, :] = tokens[...].astype(F32)
    entry[half:2 * half, :] = cotangent[...].astype(F32) * live

    barrier = pltpu.get_barrier_semaphore()
    for d in range(1, C):
        pl.semaphore_signal(barrier, inc=1, device_id={"col": (c + d) % C}, device_id_type=MESH)
    for d in range(1, R):
        pl.semaphore_signal(barrier, inc=1, device_id={"row": (r + d) % R}, device_id_type=MESH)
    pl.semaphore_wait(barrier, C - 1 + R - 1)

    base_e = ids.take(C)

    def features(j):
        return pl.ds(pl.multiple_of(j * Dc, Dc), Dc)

    for d in range(1, C):
        peer = (c + d) % C
        send(entry.at[:, features(peer)], ent.at[c], base_e + d, col=peer)
    ent[c] = entry[:, features(c)]

    outs = []

    def emit(src, dst):
        one = pltpu.make_async_copy(src, dst, osem.at[len(outs)])
        one.start()
        outs.append(one)

    def stat_send(u, value):
        base = ids.take(C)
        stats[u, c] = value
        for d in range(1, C):
            send(stats.at[u, c], stats.at[u, c], base + d, col=(c + d) % C)
        return base

    def stat_sum(u, base):
        for d in range(1, C):
            frm = (c + C - d) % C
            copy(stats.at[u, frm], stats.at[u, frm], base + d, col=frm).wait_recv()
        return jnp.sum(stats[u], axis=0)

    def order():
        return list(range(nk - 1, 0, -1)) + [0]

    def rs_core(u, chunk, m, base):
        core_s[u, m] = chunk(chip_peer(m) * 2 + (1 - core)).astype(BF)
        send(core_s.at[u, m], core_r.at[u, m], base + m, col=sib)

    def rs_own(u, chunk, m, base):
        part = chunk(chip_peer(m) * 2 + core)
        copy(core_s.at[u, m], core_r.at[u, m], base + m, col=sib).wait_recv()
        return part + core_r[u, m].astype(F32)

    def rs_start(u, chunk, later=False):
        base = ids.take(2 * nk)
        ms = order()
        rs_core(u, chunk, ms[0], base)
        total = None
        for i, m in enumerate(ms):
            if i + 1 < nk:
                rs_core(u, chunk, ms[i + 1], base)
            total = rs_own(u, chunk, m, base)
            if m:
                chip_s[u, m] = total.astype(BF)
            if m and not later:
                send(chip_s.at[u, m], chip_r.at[u, m], base + nk + m, col=chip_peer(m) * 2 + core)
        return base, total

    def rs_send(u, base):
        for m in order()[:-1]:
            send(chip_s.at[u, m], chip_r.at[u, m], base + nk + m, col=chip_peer(m) * 2 + core)

    def rs_end(u, base, total):
        for m in order()[:-1]:
            copy(chip_s.at[u, m], chip_r.at[u, m], base + nk + m, col=chip_peer(m) * 2 + core).wait_recv()
            total = total + chip_r[u, m].astype(F32)
        return total

    def ag_start(buf):
        base = ids.take(2 * nk)
        for m in order()[:-1]:
            send(buf.at[c], buf.at[c], base + m, col=chip_peer(m) * 2 + core)
        send(buf.at[c], buf.at[c], base, col=sib)
        return base

    def ag_each(buf, base, use):
        use(c)
        copy(buf.at[sib], buf.at[sib], base, col=sib).wait_recv()
        use(sib)
        for m in range(1, nk):
            peer = chip_peer(m) * 2
            mine, other = peer + core, peer + 1 - core
            copy(buf.at[mine], buf.at[mine], base + m, col=mine).wait_recv()
            send(buf.at[mine], buf.at[mine], base + nk + m, col=sib)
            use(mine)
            copy(buf.at[other], buf.at[other], base + nk + m, col=sib).wait_recv()
            use(other)

    def row_scatter(u, value_ref):
        base = ids.take(R)
        for d in range(1, R):
            peer = (r + d) % R
            row_s[u, d] = value_ref[pl.ds(pl.multiple_of(peer * Tr, Tr), Tr), :].astype(BF)
            send(row_s.at[u, d], row_r.at[u, d], base + d, row=peer)
        return base

    def row_sum(u, base, value_ref):
        total = value_ref[pl.ds(pl.multiple_of(r * Tr, Tr), Tr), :]
        for d in range(1, R):
            copy(row_s.at[u, d], row_r.at[u, d], base + d, row=(r + d) % R).wait_recv()
            total = total + row_r[u, d].astype(F32)
        return total

    def row_gather_start(buf):
        base = ids.take(R)
        for d in range(1, R):
            send(buf.at[r], buf.at[r], base + d, row=(r + d) % R)
        return base

    def row_gather_end(buf, base):
        for d in range(1, R):
            frm = (r + R - d) % R
            copy(buf.at[frm], buf.at[frm], base + d, row=frm).wait_recv()

    def lanes(j):
        return pl.ds(pl.multiple_of(j * Hc, Hc), Hc)

    gain0, gain1 = gain[0:1, :], gain[1:2, :]
    own = pl.ds(pl.multiple_of(r * Tr, Tr), Tr)

    for d in range(1, C):
        frm = (c + C - d) % C
        copy(entry.at[:, features(frm)], ent.at[frm], base_e + d, col=frm).wait_recv()
    first = lax.broadcasted_iota(jnp.int32, (2 * half, Dc), 0) < half
    tok_rows, top_rows = [], []
    for i in range(C // 2):
        low, high = ent[2 * i], ent[2 * i + 1]
        tok_rows.append(jnp.where(first, low, pltpu.roll(high, half, 0)))
        top_rows.append(jnp.where(first, pltpu.roll(low, half, 0), high))
    tok_own = jnp.concatenate(tok_rows, axis=0)
    top = jnp.concatenate(top_rows, axis=0)
    tokx[r] = tok_own.astype(BF)
    b_tok = row_gather_start(tokx)
    topx[r] = top.astype(BF)
    b_top = row_gather_start(topx)
    row_gather_end(tokx, b_tok)

    tok = tokx[...].reshape(T, Dc).astype(F32)
    s0 = stat_send(0, to_row(jnp.sum(tok * tok, axis=1, keepdims=True)))
    xa[0] = (tok * gain0).astype(BF)
    w_up0.wait()
    base, total = rs_start(0, lambda j: dot_nn(xa[0], up[0, :, lanes(j)]))
    row_gather_end(topx, b_top)
    gb[1] = topx[...].reshape(T, Dc)
    emit(gb.at[1], gradb_o.at[1])
    w_down1.wait()
    base_d, total_d = rs_start(1, lambda j: dot_nt(gb[1], down[1, lanes(j), :]), later=True)
    dh_v[...] = total_d
    rstd0 = lax.rsqrt(to_column(stat_sum(0, s0)) / D + epsilon_norm)
    stream_v[0] = rstd0
    normed_v[0] = (tok * rstd0[:, 0:1] * gain0).astype(BF)
    normed_t[0] = jnp.transpose(normed_v[0])
    emit(normed_t.at[0], normed_o.at[0])
    pre = rs_end(0, base, total) * rstd0[:, 0:1]
    value, slope = gelu_parts(pre)
    hid[0, c] = value.astype(BF)
    a0 = ag_start(hid.at[0])
    pre_v[0] = pre
    slope_v[0] = slope

    w_down0.wait()
    acc[...] = jnp.zeros_like(acc)

    def use_hidden(j):
        acc[...] += dot_nn(hid[0, j], down[0, lanes(j), :])

    ag_each(hid.at[0], a0, use_hidden)
    b = row_scatter(0, acc)
    rs_send(1, base_d)
    stream1 = tokx[r].astype(F32) + row_sum(0, b, acc)
    rowx[0, r] = (stream1 * gain1).astype(BF)
    b = row_gather_start(rowx.at[0])
    for j in range(C):
        hid_t[0, j] = jnp.transpose(hid[0, j])
    emit(hid_t.at[0], hid_o.at[0])
    dh_v[...] = rs_end(1, base_d, dh_v[...])
    w_up1.wait()
    row_gather_end(rowx.at[0], b)

    xa[1] = rowx[0].reshape(T, Dc)
    raw = xa[1].astype(F32) / gain1
    s1 = stat_send(1, to_row(jnp.sum(raw * raw, axis=1, keepdims=True)))
    base, total = rs_start(2, lambda j: dot_nn(xa[1], up[1, :, lanes(j)]))
    rstd1 = lax.rsqrt(to_column(stat_sum(1, s1)) / D + epsilon_norm)
    stream_v[1] = rstd1
    normed_v[1] = (xa[1].astype(F32) * rstd1[:, 0:1]).astype(BF)
    normed_t[1] = jnp.transpose(normed_v[1])
    emit(normed_t.at[1], normed_o.at[1])
    pre = rs_end(2, base, total) * rstd1[:, 0:1]
    value, slope = gelu_parts(pre)
    hid[1, c] = value.astype(BF)

    def backward(l, dhidden, pre, slope, stream_own, grad_above, gain_l, u):
        rounded = (dhidden * slope).astype(BF)
        dpre[l, c] = rounded
        a = ag_start(dpre.at[l])
        s = stat_send(2 + u, to_row(jnp.sum(rounded.astype(F32) * pre, axis=1, keepdims=True)))
        acc[...] = jnp.zeros_like(acc)

        def use(j):
            acc[...] += dot_nt(dpre[l, j], up[l, :, lanes(j)])

        ag_each(dpre.at[l], a, use)
        b = row_scatter(1 + u, acc)
        inner[u, r] = stat_sum(2 + u, s)
        bi = row_gather_start(inner.at[u])
        emit(dpre.at[l], dpre_o.at[l])
        a_late = ag_start(hid.at[1]) if l == 1 else None
        dnormed = row_sum(1 + u, b, acc)
        row_gather_end(inner.at[u], bi)
        stream_v[2 + u] = to_column(jnp.sum(inner[u], axis=0))
        inner_own = stream_v[2 + u, own, :][:, 0:1] / D
        rstd_own = stream_v[l, own, :][:, 0:1]
        unit = stream_own * rstd_own
        gains[l, r] = jnp.broadcast_to(jnp.sum(dnormed * unit, axis=0, keepdims=True), (8, Dc))
        bg = row_gather_start(gains.at[l])
        return grad_above + rstd_own * (dnormed * gain_l - unit * inner_own), a_late, bg

    grad1, a_late, bg1 = backward(1, dh_v[...], pre, slope, stream1, top, gain1, 0)
    rowx[1, r] = grad1.astype(BF)
    b = row_gather_start(rowx.at[1])

    def turn(j):
        hid_t[1, j] = jnp.transpose(hid[1, j])

    row_gather_end(rowx.at[1], b)
    gb[0] = rowx[1].reshape(T, Dc)
    emit(gb.at[0], gradb_o.at[0])
    base, total = rs_start(3, lambda j: dot_nt(gb[0], down[0, lanes(j), :]))
    ag_each(hid.at[1], a_late, turn)
    emit(hid_t.at[1], hid_o.at[1])
    dhidden = rs_end(3, base, total)
    grad0, _, bg0 = backward(0, dhidden, pre_v[0], slope_v[0], tokx[r].astype(F32), grad1, gain0, 1)

    fin_s[...] = grad0.reshape(C // 2, 2 * half, Dc)
    base_x = ids.take(C)
    for d in range(1, C):
        peer = (c + d) % C
        send(fin_s.at[peer // 2], fin_r.at[c], base_x + d, col=peer)
    fin_r[c] = fin_s[k]
    for l, bg in ((1, bg1), (0, bg0)):
        row_gather_end(gains.at[l], bg)
        gsum_o[l:l + 1, :] = jnp.sum(gains[l], axis=0)[0:1]
    for d in range(1, C):
        frm = (c + C - d) % C
        copy(fin_s.at[k], fin_r.at[frm], base_x + d, col=frm).wait_recv()
    upper = core == 1
    for j in range(C):
        block = fin_r[j]
        block = jnp.where(upper, pltpu.roll(block, half, 0), block)
        grad_o[:, j * Dc:(j + 1) * Dc] = block[0:half].astype(BF)
    for one in sends:
        one.wait_send()
    for one in outs:
        one.wait()


def run_layers(R, C, tokens, cotangent, counts, gain, up, down):
    L, Dc, H = up.shape
    half = tokens.shape[0]
    T = half * R * C
    Hc, Tr, nk = H // C, T // R, C // 2
    n = sem_total(R, C)
    any_spec = pl.BlockSpec(memory_space=pl.ANY)
    vm = pl.BlockSpec(memory_space=pltpu.VMEM)
    S = jax.ShapeDtypeStruct
    flops = 2 * T * Dc * H * 7
    return pl.pallas_call(
        functools.partial(layers_kernel, R, C),
        out_shape=(S((L, Dc, T), BF), S((L, T, Dc), BF), S((L, C, Hc, T), BF), S((L, C, T, Hc), BF),
                   S((half, C * Dc), BF), S((L, Dc), F32)),
        in_specs=[vm, vm, pl.BlockSpec(memory_space=pltpu.SMEM), vm, any_spec, any_spec],
        out_specs=(any_spec, any_spec, any_spec, any_spec, vm, vm),
        scratch_shapes=[
            pltpu.VMEM(up.shape, BF), pltpu.VMEM(down.shape, BF),
            pltpu.VMEM((L, Dc, T), BF), pltpu.VMEM((L, C, Hc, T), BF),
            pltpu.VMEM((2 * half, C * Dc), F32),
            pltpu.VMEM((C, 2 * half, Dc), F32), pltpu.VMEM((R, Tr, Dc), BF), pltpu.VMEM((R, Tr, Dc), BF),
            pltpu.VMEM((C // 2, 2 * half, Dc), F32), pltpu.VMEM((C, 2 * half, Dc), F32),
            pltpu.VMEM((L, R, 8, Dc), F32),
            pltpu.VMEM((L, T, Dc), BF), pltpu.VMEM((L, T, Dc), BF),
            pltpu.VMEM((L, C, T, Hc), BF), pltpu.VMEM((L, C, T, Hc), BF),
            pltpu.VMEM((4, nk, T, Hc), BF), pltpu.VMEM((4, nk, T, Hc), BF),
            pltpu.VMEM((4, nk, T, Hc), BF), pltpu.VMEM((4, nk, T, Hc), BF),
            pltpu.VMEM((T, Dc), F32),
            pltpu.VMEM((4, C, 8, T), F32), pltpu.VMEM((2, R, 8, T), F32),
            pltpu.VMEM((3, R, Tr, Dc), BF), pltpu.VMEM((3, R, Tr, Dc), BF),
            pltpu.VMEM((2, R, Tr, Dc), BF),
            pltpu.VMEM((L, T, Dc), BF),
            pltpu.VMEM((1, T, Hc), F32), pltpu.VMEM((1, T, Hc), F32), pltpu.VMEM((T, Hc), F32),
            pltpu.VMEM((4, T, 128), F32),
            pltpu.SemaphoreType.DMA((4,)), pltpu.SemaphoreType.DMA((8,)),
            pltpu.SemaphoreType.DMA((n,)), pltpu.SemaphoreType.DMA((n,)),
        ],
        compiler_params=pltpu.CompilerParams(collective_id=0, has_side_effects=True,
                                             vmem_limit_bytes=56 * 1024 * 1024),
        cost_estimate=pl.CostEstimate(flops=flops, bytes_accessed=2 * up.size * 4, transcendentals=0),
        name="layers",
    )(tokens, cotangent, counts, gain, up, down)


def grads_kernel(normed, gradb, hid, dpre, token_in, gain_in, up_g, down_g, token_g, gain_g):
    up_g[0] = dot_nn(normed[0], dpre[0, 0])
    down_g[0] = dot_nn(hid[0, 0], gradb[0])

    @pl.when((pl.program_id(0) == 0) & (pl.program_id(1) == 0))
    def _():
        token_g[...] = token_in[...]
        gain_g[...] = gain_in[...]


def run_grads(normed, gradb, hid, dpre, token, gain):
    L, T, Dc = gradb.shape
    _, C, _, Hc = dpre.shape
    S = jax.ShapeDtypeStruct
    token_spec = pl.BlockSpec(token.shape, lambda l, j: (0, 0))
    gain_spec = pl.BlockSpec(gain.shape, lambda l, j: (0, 0))
    return pl.pallas_call(
        grads_kernel,
        grid=(L, C),
        out_shape=(S((L, Dc, C * Hc), F32), S((L, C * Hc, Dc), F32), S(token.shape, BF), S(gain.shape, F32)),
        in_specs=[pl.BlockSpec((1, Dc, T), lambda l, j: (l, 0, 0)),
                  pl.BlockSpec((1, T, Dc), lambda l, j: (l, 0, 0)),
                  pl.BlockSpec((1, 1, Hc, T), lambda l, j: (l, j, 0, 0)),
                  pl.BlockSpec((1, 1, T, Hc), lambda l, j: (l, j, 0, 0)),
                  token_spec, gain_spec],
        out_specs=(pl.BlockSpec((1, Dc, Hc), lambda l, j: (l, 0, j)),
                   pl.BlockSpec((1, Hc, Dc), lambda l, j: (l, j, 0)),
                   token_spec, gain_spec),
        compiler_params=pltpu.CompilerParams(vmem_limit_bytes=60 * 1024 * 1024),
        cost_estimate=pl.CostEstimate(flops=4 * L * T * Dc * C * Hc, bytes_accessed=8 * L * Dc * C * Hc,
                                      transcendentals=0),
        name="grads",
    )(normed, gradb, hid, dpre, token, gain)


def on_device(R, C, tokens, counts, cotangent, up_weight, down_weight, norm_gain):
    normed, gradb, hid, dpre, token, gain = run_layers(R, C, tokens, cotangent, counts, norm_gain,
                                                       up_weight, down_weight)
    up_g, down_g, token_grad, gain_grad = run_grads(normed, gradb, hid, dpre, token, gain)
    return token_grad, up_g, down_g, gain_grad


def solution(mesh):
    R, C = mesh.shape["row"], mesh.shape["col"]
    return jax.shard_map(
        functools.partial(on_device, R, C),
        mesh=mesh,
        in_specs=(P(("row", "col"), None), P(("row", "col")), P(("row", "col"), None),
                  P(None, "col", "row"), P(None, "row", "col"), P(None, "col")),
        out_specs=(P(("row", "col"), None), P(None, "col", "row"), P(None, "row", "col"), P(None, "col")),
        check_vma=False,
    )
```
